32 devices in a mesh: gz: 4 (over z), gy: 2 (over y), gx: 4 (over x, core).
Axes of the slice: x: 2, y: 2, z: 4, core: 2. Of those that a mesh axis runs over, the one named last changes fastest.
Arguments:
- positions: float32 [3, 12, 6, 12, 128], P(None, 'gz', 'gy', 'gx'), may hold values from 0 to 1
- velocities: float32 [3, 12, 6, 12, 128], P(None, 'gz', 'gy', 'gx'), may hold values from -6 to 6
- counts: int32 [12, 6, 12], P('gz', 'gy', 'gx'), may hold values from 64 to 128
- bonds: int32 [2, 12, 6, 12, 128], P(None, 'gz', 'gy', 'gx'), may hold values from 0 to 127
- plan_z: int32 [4], replicated, may hold values from 0 to 2
- plan_y: int32 [4, 2], replicated, may hold values from 0 to 2
- plan_x: int32 [4, 2, 4], replicated, may hold values from 0 to 2
Outputs:
- forces_first: float32 [3, 12, 6, 12, 128], P(None, 'gz', 'gy', 'gx')
- moved_positions: float32 [3, 20, 10, 20, 128], P(None, 'gz', 'gy', 'gx')
- moved_forces: float32 [3, 20, 10, 20, 128], P(None, 'gz', 'gy', 'gx')
The draws below stay inside these ranges and needn't reach their ends.
Inputs may be any that keep to these rules, and one draw needn't show every extreme that they name: `counts`: bead b of a cell is present when b is less than the cell's count. `bonds`: both ends of a bond are bead places of the bond's own cell; a bond counts only when both ends are present. `plan_z`: entry i is the number of cells by which the boundary between brick planes i and i + 1 (the last with plane 0) moves up. `plan_y`: entry (i, j) is the number of cells by which the boundary between columns j and j + 1 of plane i (the last with column 0) moves up. `plan_x`: entry (i, j, k) is the number of cells by which the boundary between bricks k and k + 1 of column (i, j) (the last with brick 0) moves up.
All inputs are finite; a program needn't handle non-finite values.
Results may differ from the reference program's by a relative error of at most 0.0001.
Values sent between devices are 32-bit elements; how exact they have to be, the bound alone decides.
A program may use at most 64 MiB of HBM per device.

```python
import jax
import jax.numpy as jnp
from jax import lax

CELLS = 3
BEADS = 128
BONDS = 128
SLOTS = 5
NZ = 12
NY = 6
NX = 12
MZ = 20
MY = 10
MX = 20
N_GZ = 4
N_GY = 2
N_GX = 4


def plant(entries, stream_key, least, largest):
    place = [jax.random.randint(jax.random.fold_in(stream_key, axis), (), 0, length) for axis, length in enumerate(entries.shape)]
    widest = entries.shape.index(max(entries.shape))
    neighbour = place[:widest] + [(place[widest] + 1) % entries.shape[widest]] + place[widest + 1:]
    return entries.at[tuple(place)].set(least).at[tuple(neighbour)].set(largest)


def block_scale(key, shape, shards, least, high):
    def one(dim, parts):
        heights = jax.random.uniform(jax.random.fold_in(jax.random.fold_in(key, 6), dim), (parts,), jnp.float32, least / len(shards), high / len(shards))
        return jnp.repeat(jnp.exp(heights), shape[dim] // parts).reshape((-1,) + (1,) * (len(shape) - dim - 1))

    factor_of = one(*shards[0])
    for cut in shards[1:]:
        factor_of = factor_of * one(*cut)
    return factor_of


def scatter_about(own_key, shape, scale, most, shards=(), kind=jnp.bfloat16):
    values = jax.random.normal(own_key, shape, jnp.float32) * scale
    if len(shards) > 0:
        values = block_scale(own_key, shape, shards, -0.22, 0.18) * values
    return jnp.clip(values, min=-most, max=most).astype(kind)


def setup_inputs(seed: int = 0) -> dict:
    keys = jax.random.split(jax.random.key(seed), 8)
    return {
        "positions": jnp.clip(1.0 * jax.random.uniform(keys[0], (3, NZ, NY, NX, BEADS), jnp.float32) ** block_scale(keys[0], (3, NZ, NY, NX, BEADS), ((1, 4), (2, 2), (3, 4)), -0.2, 0.2), 0.0, 1.0),
        "velocities": scatter_about(keys[1], (3, NZ, NY, NX, BEADS), 1.0, 6.0, ((1, 4), (2, 2), (3, 4)), jnp.float32),
        "counts": plant(jax.random.randint(keys[2], (NZ, NY, NX), BEADS // 2, BEADS + 1), jax.random.fold_in(keys[2], 1), BEADS // 2, BEADS).astype(jnp.int32),
        "bonds": plant(jax.random.randint(keys[3], (2, NZ, NY, NX, BONDS), 0, BEADS), jax.random.fold_in(keys[3], 1), 0, BEADS - 1).astype(jnp.int32),
        "plan_z": plant(jax.random.randint(keys[4], (N_GZ,), 0, 3), jax.random.fold_in(keys[4], 1), 0, 2).astype(jnp.int32),
        "plan_y": plant(jax.random.randint(keys[5], (N_GZ, N_GY), 0, 3), jax.random.fold_in(keys[5], 1), 0, 2).astype(jnp.int32),
        "plan_x": plant(jax.random.randint(keys[6], (N_GZ, N_GY, N_GX), 0, 3), jax.random.fold_in(keys[6], 1), 0, 2).astype(jnp.int32),
    }


STRENGTH = 0.3
SPREAD = 0.6
BOND_STIFF = 1.0
STEP_DT = 0.2
ALL_OFFSETS = [(along_z, along_y, along_x) for along_z in (-1, 0, 1) for along_y in (-1, 0, 1) for along_x in (-1, 0, 1)]


def pair_block(own_beads, own_alive, partner, partner_alive, offset):
    offset_vec = jnp.array(offset, dtype=jnp.float32).reshape(3, 1, 1, 1)
    separation = own_beads[:, :, :, None] - partner[:, :, None, :] - offset_vec
    distance = jnp.sum(separation * separation, axis=0)
    weight = STRENGTH * jnp.exp(-distance / SPREAD) * own_alive[:, :, None] * partner_alive[:, None, :]
    return jnp.sum(weight[None] * separation, axis=3)


def pair_forces(coords, living):
    padded = jnp.concatenate([coords[:, -1:], coords, coords[:, :1]], axis=1)
    padded_live = jnp.concatenate([living[-1:], living, living[:1]], axis=0)

    def plane_forces(plane_index):
        three_planes = lax.dynamic_slice_in_dim(padded, plane_index, 3, 1)
        three_live = lax.dynamic_slice_in_dim(padded_live, plane_index, 3, 0)
        own_beads = three_planes[:, 1].reshape(3, -1, BEADS)
        own_alive = three_live[1].reshape(-1, BEADS)
        summed = jnp.zeros_like(own_beads)
        for offset in ALL_OFFSETS:
            partner = jnp.roll(three_planes[:, 1 + offset[0]], (-offset[1], -offset[2]), axis=(1, 2)).reshape(3, -1, BEADS)
            partner_alive = jnp.roll(three_live[1 + offset[0]], (-offset[1], -offset[2]), axis=(0, 1)).reshape(-1, BEADS)
            summed = summed + pair_block(own_beads, own_alive, partner, partner_alive, offset)
        return summed.reshape(3, NY, NX, BEADS)

    planes = lax.map(plane_forces, jnp.arange(NZ, dtype=jnp.int32))
    return jnp.moveaxis(planes, 0, 1)


def bond_forces(coords, living, bonds):
    flat_coords = coords.reshape(3, -1, BEADS)
    flat_alive = living.reshape(-1, BEADS)
    head_ends = bonds[0].reshape(-1, BONDS)
    tail_ends = bonds[1].reshape(-1, BONDS)
    head_wide = jnp.broadcast_to(head_ends[None], (3,) + head_ends.shape)
    tail_wide = jnp.broadcast_to(tail_ends[None], (3,) + tail_ends.shape)
    head_pos = jnp.take_along_axis(flat_coords, head_wide, axis=2)
    tail_pos = jnp.take_along_axis(flat_coords, tail_wide, axis=2)
    bonded = jnp.take_along_axis(flat_alive, head_ends, axis=1) * jnp.take_along_axis(flat_alive, tail_ends, axis=1)
    tension = BOND_STIFF * bonded[None] * (tail_pos - head_pos)
    cell_ids = jnp.arange(flat_coords.shape[1], dtype=jnp.int32)[:, None]
    summed = jnp.zeros_like(flat_coords)
    summed = summed.at[:, cell_ids, head_ends].add(tension)
    summed = summed.at[:, cell_ids, tail_ends].add(-tension)
    return summed.reshape(coords.shape)


def all_forces(coords, living, bonds):
    return pair_forces(coords, living) + bond_forces(coords, living, bonds)


def placement(plan_table, extent):
    owner_count = plan_table.shape[-1]
    lowered = jnp.roll(plan_table, 1, axis=-1)
    filled = CELLS + plan_table - lowered
    owners = jnp.arange(owner_count, dtype=jnp.int32)
    slot_index = jnp.arange(SLOTS, dtype=jnp.int32)
    first_cell = owners * CELLS + lowered
    target = (first_cell[..., None] + slot_index) % extent
    usable = slot_index < filled[..., None]
    grid_index = jnp.arange(extent, dtype=jnp.int32)
    matches = (target[..., None] == grid_index) & usable[..., None]
    return matches.astype(jnp.float32)


def relayout(carried, plan_z, plan_y, plan_x):
    components = carried.shape[0]
    along_z = placement(plan_z, NZ)
    step_one = jnp.einsum('htz,czyxb->chtyxb', along_z, carried, precision=lax.Precision.HIGHEST)
    along_y = placement(plan_y, NY)
    step_two = jnp.einsum('hjty,chsyxb->chsjtxb', along_y, step_one, precision=lax.Precision.HIGHEST)
    along_x = placement(plan_x, NX)
    step_three = jnp.einsum('hjgux,chsjtxb->chsjtgub', along_x, step_two, precision=lax.Precision.HIGHEST)
    return step_three.reshape(components, MZ, MY, MX, BEADS)


def reference(positions, velocities, counts, bonds, plan_z, plan_y, plan_x):
    living = (jnp.arange(BEADS, dtype=jnp.int32) < counts[..., None]).astype(jnp.float32)
    forces_first = all_forces(positions, living, bonds)
    stepped = positions + STEP_DT * velocities + (0.5 * STEP_DT * STEP_DT) * forces_first
    forces_next = all_forces(stepped, living, bonds)
    carried = jnp.concatenate([stepped * living[None], forces_next], axis=0)
    moved = relayout(carried, plan_z, plan_y, plan_x)
    return forces_first, moved[:3], moved[3:]
```

```python
import functools
import math

import jax
import jax.numpy as jnp
from jax import lax
from jax.experimental import pallas as pl
from jax.experimental.pallas import tpu as pltpu
from jax.sharding import PartitionSpec as P

STRENGTH = 0.3
SPREAD = 0.6
BOND_STIFF = 1.0
STEP_DT = 0.2
FAR_AWAY = 1000.0
UNIT = math.sqrt(1.0 / (SPREAD * math.log(2.0)))
ROWS = 16


def from_behind(block, axis, distance):
    devices = range(lax.axis_size(axis))
    route = [((i - distance) % len(devices), i) for i in devices]
    return lax.ppermute(block, axis, route)


def split_three(values):
    high = values.astype(jnp.bfloat16)
    rest = values - high.astype(jnp.float32)
    middle = rest.astype(jnp.bfloat16)
    low = (rest - middle.astype(jnp.float32)).astype(jnp.bfloat16)
    return high, middle, low


def bond_kernel(side, counts_ref, bonds_ref, lap_ref):
    beads = lap_ref.shape[-1]
    bond_count = bonds_ref.shape[-1]

    def one_row(row, carry):
        z, y = row // side, lax.rem(row, side)
        bead = lax.broadcasted_iota(jnp.int32, (beads, bond_count), 0)
        for x in range(side):
            count = counts_ref[z, y, x]
            head = bonds_ref[0, z, y, x : x + 1, :]
            tail = bonds_ref[1, z, y, x : x + 1, :]
            alive = ((head < count) & (tail < count)).astype(jnp.float32)
            ends = jnp.where(bead == head, alive, 0.0) - jnp.where(bead == tail, alive, 0.0)
            ends = ends.astype(jnp.bfloat16)
            lap_ref[row, x] = lax.dot_general(
                ends, ends, (((1,), (1,)), ((), ())), preferred_element_type=jnp.float32
            ).astype(jnp.bfloat16)
        return carry

    lax.fori_loop(0, side * side, one_row, 0)


def force_kernel(side, counts_ref, ext_ref, lap_ref, out_ref, grid_ref, own_ref, sum_ref):
    beads = ext_ref.shape[-1]
    wide = side + 2
    padded = grid_ref.shape[3]

    shape = (wide, wide, wide, beads)
    for k in range(3):
        shift = lax.broadcasted_iota(jnp.int32, shape, k).astype(jnp.float32)
        grid_ref[k, :, :, 0:wide, :] = (ext_ref[k] + shift) * UNIT

    def one_row(row, carry):
        z, y = row // side, lax.rem(row, side)
        tile = jnp.concatenate(
            [grid_ref[k, z + 1, y + 1] for k in range(3)], axis=0
        )
        columns = tile.T
        for k in range(3):
            for x in range(side):
                place = k * padded + x + 1
                own_ref[k * side + x] = jnp.broadcast_to(
                    columns[:, place : place + 1], (beads, beads)
                )
        for x in range(side):
            count = counts_ref[z, y, x]

            def one_block(i, inner):
                rows = pl.ds(pl.multiple_of(i * ROWS, ROWS), ROWS)
                own = [own_ref[k * side + x, rows, :] for k in range(3)]
                total = [jnp.zeros((ROWS, beads), jnp.float32) for _ in range(3)]
                for dz in range(3):
                    for dy in range(3):
                        for dx in range(3):
                            apart = [
                                own[k]
                                - grid_ref[k, z + dz, y + dy, x + dx : x + dx + 1, :]
                                for k in range(3)
                            ]
                            distance = (
                                apart[0] * apart[0] + apart[1] * apart[1] + apart[2] * apart[2]
                            )
                            weight = jnp.exp2(-distance)
                            total = [total[k] + weight * apart[k] for k in range(3)]
                for k in range(3):
                    sum_ref[k * side + x, rows, :] = total[k]
                return inner

            lax.fori_loop(0, (count + (ROWS - 1)) // ROWS, one_block, 0)
        lane = lax.broadcasted_iota(jnp.int32, (1, beads), 1)
        for x in range(side):
            count = counts_ref[z, y, x]
            high, middle, low = split_three(
                jnp.concatenate(
                    [grid_ref[k, z + 1, y + 1, x + 1 : x + 2, :] for k in range(3)]
                    + [jnp.zeros((5, beads), jnp.float32)],
                    axis=0,
                )
            )
            lap = lap_ref[row, x]
            bond = (
                jnp.dot(low, lap, preferred_element_type=jnp.float32)
                + jnp.dot(middle, lap, preferred_element_type=jnp.float32)
                + jnp.dot(high, lap, preferred_element_type=jnp.float32)
            )
            for k in range(3):
                pair = jnp.sum(sum_ref[k * side + x].T, axis=0, keepdims=True)
                force = (STRENGTH / UNIT) * pair - (BOND_STIFF / UNIT) * bond[k : k + 1]
                out_ref[k, z, y, x : x + 1, :] = jnp.where(lane < count, force, 0.0)
        return carry

    lax.fori_loop(0, side * side, one_row, 0)


def bond_matrices(counts, bonds, beads):
    side = counts.shape[0]
    return pl.pallas_call(
        functools.partial(bond_kernel, side),
        out_shape=jax.ShapeDtypeStruct((side * side, side, beads, beads), jnp.bfloat16),
        in_specs=[
            pl.BlockSpec(memory_space=pltpu.SMEM),
            pl.BlockSpec(memory_space=pltpu.VMEM),
        ],
        out_specs=pl.BlockSpec(memory_space=pltpu.VMEM),
        compiler_params=pltpu.CompilerParams(vmem_limit_bytes=40 * 1024 * 1024),
        name="bond_matrices",
    )(counts, bonds)


def local_forces(extended, counts, laps):
    side = counts.shape[0]
    beads = extended.shape[-1]
    wide = side + 2
    padded = -(-wide // 8) * 8
    return pl.pallas_call(
        functools.partial(force_kernel, side),
        out_shape=jax.ShapeDtypeStruct((3, side, side, side, beads), jnp.float32),
        in_specs=[
            pl.BlockSpec(memory_space=pltpu.SMEM),
            pl.BlockSpec(memory_space=pltpu.VMEM),
            pl.BlockSpec(memory_space=pltpu.VMEM),
        ],
        out_specs=pl.BlockSpec(memory_space=pltpu.VMEM),
        scratch_shapes=[
            pltpu.VMEM((3, wide, wide, padded, beads), jnp.float32),
            pltpu.VMEM((3 * side, beads, beads), jnp.float32),
            pltpu.VMEM((3 * side, beads, beads), jnp.float32),
        ],
        compiler_params=pltpu.CompilerParams(vmem_limit_bytes=40 * 1024 * 1024),
        name="cell_forces",
    )(counts, extended, laps)


def halo_extend(parked):
    grown = parked
    for dim, axis in ((1, "gz"), (2, "gy"), (3, "gx")):
        size = grown.shape[dim]
        below = from_behind(lax.slice_in_dim(grown, size - 1, size, axis=dim), axis, 1)
        above = from_behind(lax.slice_in_dim(grown, 0, 1, axis=dim), axis, -1)
        grown = jnp.concatenate([below, grown, above], axis=dim)
    return grown


def pick_entry(plan_table, position):
    matched = jnp.arange(plan_table.shape[0], dtype=jnp.int32) == position
    return jnp.sum(
        jnp.where(matched.reshape((-1,) + (1,) * (plan_table.ndim - 1)), plan_table, 0), axis=0
    )


def hand_over(blocks, arrival, which_axis, lowered, raised, side_cells):
    joined = jnp.concatenate([blocks, arrival, jnp.zeros_like(arrival)], axis=which_axis)
    kept_part = lax.dynamic_slice_in_dim(joined, lowered, side_cells + 2, axis=which_axis)
    filled = side_cells + raised - lowered
    usable = (jnp.arange(side_cells + 2, dtype=jnp.int32) < filled).astype(jnp.float32)
    shape_list = [1] * blocks.ndim
    shape_list[which_axis] = side_cells + 2
    return kept_part * usable.reshape(shape_list)


def on_device(positions, velocities, counts, bonds, plan_z, plan_y, plan_x):
    side_cells = positions.shape[1]
    bead_count = positions.shape[-1]
    living = (jnp.arange(bead_count, dtype=jnp.int32) < counts[..., None]).astype(jnp.float32)
    laps = bond_matrices(counts, bonds, bead_count)
    parked = jnp.where(living[None] > 0, positions, FAR_AWAY)
    forces_first = local_forces(halo_extend(parked), counts, laps)
    stepped = positions + STEP_DT * velocities + 0.5 * STEP_DT * STEP_DT * forces_first
    parked = jnp.where(living[None] > 0, stepped, FAR_AWAY)
    forces_next = local_forces(halo_extend(parked), counts, laps)
    carried = jnp.concatenate([stepped * living[None], forces_next], axis=0)
    plane_index = lax.axis_index("gz")
    column_index = lax.axis_index("gy")
    brick_index = lax.axis_index("gx")
    plane_total = lax.axis_size("gz")
    column_total = lax.axis_size("gy")
    brick_total = lax.axis_size("gx")
    lowered_z = pick_entry(plan_z, (plane_index + plane_total - 1) % plane_total)
    raised_z = pick_entry(plan_z, plane_index)
    plane_row = pick_entry(plan_y, plane_index)
    lowered_y = pick_entry(plane_row, (column_index + column_total - 1) % column_total)
    raised_y = pick_entry(plane_row, column_index)
    column_row = pick_entry(pick_entry(plan_x, plane_index), column_index)
    lowered_x = pick_entry(column_row, (brick_index + brick_total - 1) % brick_total)
    raised_x = pick_entry(column_row, brick_index)
    arrival = from_behind(lax.slice_in_dim(carried, 0, 2, axis=1), "gz", -1)
    carried = hand_over(carried, arrival, 1, lowered_z, raised_z, side_cells)
    arrival = from_behind(lax.slice_in_dim(carried, 0, 2, axis=2), "gy", -1)
    carried = hand_over(carried, arrival, 2, lowered_y, raised_y, side_cells)
    arrival = from_behind(lax.slice_in_dim(carried, 0, 2, axis=3), "gx", -1)
    carried = hand_over(carried, arrival, 3, lowered_x, raised_x, side_cells)
    return (forces_first, carried[:3], carried[3:])


def solution(mesh):
    return jax.shard_map(
        on_device,
        mesh=mesh,
        in_specs=(
            P(None, "gz", "gy", "gx", None),
            P(None, "gz", "gy", "gx", None),
            P("gz", "gy", "gx"),
            P(None, "gz", "gy", "gx", None),
            P(),
            P(),
            P(),
        ),
        out_specs=(
            P(None, "gz", "gy", "gx", None),
            P(None, "gz", "gy", "gx", None),
            P(None, "gz", "gy", "gx", None),
        ),
        check_vma=False,
    )
```

```python
import functools
import math

import jax
import jax.numpy as jnp
from jax import lax
from jax.experimental import pallas as pl
from jax.experimental.pallas import tpu as pltpu
from jax.sharding import PartitionSpec as P

STRENGTH = 0.3
SPREAD = 0.6
BOND_STIFF = 1.0
STEP_DT = 0.2
FAR_AWAY = 1000.0
UNIT = math.sqrt(1.0 / (SPREAD * math.log(2.0)))
ROWS = 32


def from_behind(block, axis, distance):
    devices = range(lax.axis_size(axis))
    route = [((i - distance) % len(devices), i) for i in devices]
    return lax.ppermute(block, axis, route)


def split_three(values):
    high = values.astype(jnp.bfloat16).astype(jnp.float32)
    rest = values - high
    middle = rest.astype(jnp.bfloat16).astype(jnp.float32)
    return [high, middle, rest - middle]


def bond_kernel(side, counts_ref, bonds_ref, lap_ref):
    beads = lap_ref.shape[-1]
    bond_count = bonds_ref.shape[-1]

    def one_row(row, carry):
        z, y = row // side, lax.rem(row, side)
        bead = lax.broadcasted_iota(jnp.int32, (beads, bond_count), 0)
        for x in range(side):
            count = counts_ref[z, y, x]
            head = bonds_ref[0, z, y, x : x + 1, :]
            tail = bonds_ref[1, z, y, x : x + 1, :]
            alive = ((head < count) & (tail < count)).astype(jnp.float32)
            ends = jnp.where(bead == head, alive, 0.0) - jnp.where(bead == tail, alive, 0.0)
            ends = ends.astype(jnp.bfloat16)
            lap_ref[row, x] = lax.dot_general(
                ends, ends, (((1,), (1,)), ((), ())), preferred_element_type=jnp.float32
            ).astype(jnp.bfloat16)
        return carry

    lax.fori_loop(0, side * side, one_row, 0)


def force_kernel(side, counts_ref, ext_ref, lap_ref, out_ref, grid_ref, own_ref, sum_ref):
    beads = ext_ref.shape[-1]
    wide = side + 2
    padded = grid_ref.shape[3]

    shape = (wide, wide, wide, beads)
    for k in range(3):
        shift = lax.broadcasted_iota(jnp.int32, shape, k).astype(jnp.float32)
        grid_ref[k, :, :, 0:wide, :] = (ext_ref[k] + shift) * UNIT

    def one_row(row, carry):
        z, y = row // side, lax.rem(row, side)
        tile = jnp.concatenate(
            [grid_ref[k, z + 1, y + 1] for k in range(3)], axis=0
        )
        columns = tile.T
        for k in range(3):
            for x in range(side):
                place = k * padded + x + 1
                own_ref[k * side + x] = jnp.broadcast_to(
                    columns[:, place : place + 1], (beads, beads)
                )
        for x in range(side):
            count = counts_ref[z, y, x]

            def one_block(i, inner):
                rows = pl.ds(pl.multiple_of(i * ROWS, ROWS), ROWS)
                own = [own_ref[k * side + x, rows, :] for k in range(3)]
                total = [jnp.zeros((ROWS, beads), jnp.float32) for _ in range(3)]
                for dz in range(3):
                    for dy in range(3):
                        for dx in range(3):
                            apart = [
                                own[k]
                                - grid_ref[k, z + dz, y + dy, x + dx : x + dx + 1, :]
                                for k in range(3)
                            ]
                            distance = (
                                apart[0] * apart[0] + apart[1] * apart[1] + apart[2] * apart[2]
                            )
                            weight = jnp.exp2(-distance)
                            total = [total[k] + weight * apart[k] for k in range(3)]
                for k in range(3):
                    sum_ref[k * side + x, rows, :] = total[k]
                return inner

            lax.fori_loop(0, (count + (ROWS - 1)) // ROWS, one_block, 0)
        lane = lax.broadcasted_iota(jnp.int32, (1, beads), 1)
        for x in range(side):
            count = counts_ref[z, y, x]
            parts = split_three(
                jnp.concatenate(
                    [grid_ref[k, z + 1, y + 1, x + 1 : x + 2, :] for k in range(3)]
                    + [jnp.zeros((5, beads), jnp.float32)],
                    axis=0,
                )
            )
            stacked = jnp.concatenate(parts + [jnp.zeros((8, beads), jnp.float32)], axis=0)
            product = jnp.dot(
                stacked.astype(jnp.bfloat16), lap_ref[row, x], preferred_element_type=jnp.float32
            )
            bond = product[16:24] + product[8:16] + product[0:8]
            for k in range(3):
                pair = jnp.sum(sum_ref[k * side + x].T, axis=0, keepdims=True)
                force = (STRENGTH / UNIT) * pair - (BOND_STIFF / UNIT) * bond[k : k + 1]
                out_ref[k, z, y, x : x + 1, :] = jnp.where(lane < count, force, 0.0)
        return carry

    lax.fori_loop(0, side * side, one_row, 0)


def bond_matrices(counts, bonds, beads):
    side = counts.shape[0]
    return pl.pallas_call(
        functools.partial(bond_kernel, side),
        out_shape=jax.ShapeDtypeStruct((side * side, side, beads, beads), jnp.bfloat16),
        in_specs=[
            pl.BlockSpec(memory_space=pltpu.SMEM),
            pl.BlockSpec(memory_space=pltpu.VMEM),
        ],
        out_specs=pl.BlockSpec(memory_space=pltpu.VMEM),
        compiler_params=pltpu.CompilerParams(vmem_limit_bytes=40 * 1024 * 1024),
        cost_estimate=pl.CostEstimate(
            flops=2 * side**3 * beads**3, bytes_accessed=2 * side**3 * beads**2, transcendentals=0
        ),
        name="bond_matrices",
    )(counts, bonds)


def local_forces(extended, counts, laps):
    side = counts.shape[0]
    beads = extended.shape[-1]
    wide = side + 2
    padded = -(-wide // 8) * 8
    return pl.pallas_call(
        functools.partial(force_kernel, side),
        out_shape=jax.ShapeDtypeStruct((3, side, side, side, beads), jnp.float32),
        in_specs=[
            pl.BlockSpec(memory_space=pltpu.SMEM),
            pl.BlockSpec(memory_space=pltpu.VMEM),
            pl.BlockSpec(memory_space=pltpu.VMEM),
        ],
        out_specs=pl.BlockSpec(memory_space=pltpu.VMEM),
        scratch_shapes=[
            pltpu.VMEM((3, wide, wide, padded, beads), jnp.float32),
            pltpu.VMEM((3 * side, beads, beads), jnp.float32),
            pltpu.VMEM((3 * side, beads, beads), jnp.float32),
        ],
        compiler_params=pltpu.CompilerParams(vmem_limit_bytes=40 * 1024 * 1024),
        name="cell_forces",
    )(counts, extended, laps)


def halo_extend(parked):
    grown = parked
    for dim, axis in ((1, "gz"), (2, "gy"), (3, "gx")):
        size = grown.shape[dim]
        below = from_behind(lax.slice_in_dim(grown, size - 1, size, axis=dim), axis, 1)
        above = from_behind(lax.slice_in_dim(grown, 0, 1, axis=dim), axis, -1)
        grown = jnp.concatenate([below, grown, above], axis=dim)
    return grown


def pick_entry(plan_table, position):
    matched = jnp.arange(plan_table.shape[0], dtype=jnp.int32) == position
    return jnp.sum(
        jnp.where(matched.reshape((-1,) + (1,) * (plan_table.ndim - 1)), plan_table, 0), axis=0
    )


def hand_over(blocks, arrival, which_axis, lowered, raised, side_cells):
    joined = jnp.concatenate([blocks, arrival, jnp.zeros_like(arrival)], axis=which_axis)
    kept_part = lax.dynamic_slice_in_dim(joined, lowered, side_cells + 2, axis=which_axis)
    filled = side_cells + raised - lowered
    usable = (jnp.arange(side_cells + 2, dtype=jnp.int32) < filled).astype(jnp.float32)
    shape_list = [1] * blocks.ndim
    shape_list[which_axis] = side_cells + 2
    return kept_part * usable.reshape(shape_list)


def on_device(positions, velocities, counts, bonds, plan_z, plan_y, plan_x):
    side_cells = positions.shape[1]
    bead_count = positions.shape[-1]
    living = (jnp.arange(bead_count, dtype=jnp.int32) < counts[..., None]).astype(jnp.float32)
    laps = bond_matrices(counts, bonds, bead_count)
    parked = jnp.where(living[None] > 0, positions, FAR_AWAY)
    forces_first = local_forces(halo_extend(parked), counts, laps)
    stepped = positions + STEP_DT * velocities + 0.5 * STEP_DT * STEP_DT * forces_first
    parked = jnp.where(living[None] > 0, stepped, FAR_AWAY)
    forces_next = local_forces(halo_extend(parked), counts, laps)
    carried = jnp.concatenate([stepped * living[None], forces_next], axis=0)
    plane_index = lax.axis_index("gz")
    column_index = lax.axis_index("gy")
    brick_index = lax.axis_index("gx")
    plane_total = lax.axis_size("gz")
    column_total = lax.axis_size("gy")
    brick_total = lax.axis_size("gx")
    lowered_z = pick_entry(plan_z, (plane_index + plane_total - 1) % plane_total)
    raised_z = pick_entry(plan_z, plane_index)
    plane_row = pick_entry(plan_y, plane_index)
    lowered_y = pick_entry(plane_row, (column_index + column_total - 1) % column_total)
    raised_y = pick_entry(plane_row, column_index)
    column_row = pick_entry(pick_entry(plan_x, plane_index), column_index)
    lowered_x = pick_entry(column_row, (brick_index + brick_total - 1) % brick_total)
    raised_x = pick_entry(column_row, brick_index)
    arrival = from_behind(lax.slice_in_dim(carried, 0, 2, axis=1), "gz", -1)
    carried = hand_over(carried, arrival, 1, lowered_z, raised_z, side_cells)
    arrival = from_behind(lax.slice_in_dim(carried, 0, 2, axis=2), "gy", -1)
    carried = hand_over(carried, arrival, 2, lowered_y, raised_y, side_cells)
    arrival = from_behind(lax.slice_in_dim(carried, 0, 2, axis=3), "gx", -1)
    carried = hand_over(carried, arrival, 3, lowered_x, raised_x, side_cells)
    return (forces_first, carried[:3], carried[3:])


def solution(mesh):
    return jax.shard_map(
        on_device,
        mesh=mesh,
        in_specs=(
            P(None, "gz", "gy", "gx", None),
            P(None, "gz", "gy", "gx", None),
            P("gz", "gy", "gx"),
            P(None, "gz", "gy", "gx", None),
            P(),
            P(),
            P(),
        ),
        out_specs=(
            P(None, "gz", "gy", "gx", None),
            P(None, "gz", "gy", "gx", None),
            P(None, "gz", "gy", "gx", None),
        ),
        check_vma=False,
    )
```

```python
import functools
import math

import jax
import jax.numpy as jnp
from jax import lax
from jax.experimental import pallas as pl
from jax.experimental.pallas import tpu as pltpu
from jax.sharding import PartitionSpec as P

STRENGTH = 0.3
SPREAD = 0.6
BOND_STIFF = 1.0
STEP_DT = 0.2
FAR_AWAY = 1000.0
UNIT = math.sqrt(1.0 / SPREAD)
ROWS = 8


def from_behind(block, axis, distance):
    devices = range(lax.axis_size(axis))
    route = [((i - distance) % len(devices), i) for i in devices]
    return lax.ppermute(block, axis, route)


def split_three(values):
    high = values.astype(jnp.bfloat16).astype(jnp.float32)
    rest = values - high
    middle = rest.astype(jnp.bfloat16).astype(jnp.float32)
    return [high, middle, rest - middle]


def bond_kernel(side, counts_ref, bonds_ref, lap_ref):
    beads = lap_ref.shape[-1]
    bond_count = bonds_ref.shape[-1]

    def one_row(row, carry):
        z, y = row // side, lax.rem(row, side)
        bead = lax.broadcasted_iota(jnp.int32, (beads, bond_count), 0)
        for x in range(side):
            count = counts_ref[z, y, x]
            head = bonds_ref[0, z, y, x : x + 1, :]
            tail = bonds_ref[1, z, y, x : x + 1, :]
            alive = ((head < count) & (tail < count)).astype(jnp.float32)
            ends = jnp.where(bead == head, alive, 0.0) - jnp.where(bead == tail, alive, 0.0)
            ends = ends.astype(jnp.bfloat16)
            lap_ref[row, x] = lax.dot_general(
                ends, ends, (((1,), (1,)), ((), ())), preferred_element_type=jnp.float32
            ).astype(jnp.bfloat16)
        return carry

    lax.fori_loop(0, side * side, one_row, 0)


def force_kernel(side, counts_ref, ext_ref, lap_ref, out_ref, grid_ref, own_ref, sum_ref):
    beads = ext_ref.shape[-1]
    wide = side + 2
    padded = grid_ref.shape[3]

    shape = (wide, wide, wide, beads)
    for k in range(3):
        shift = lax.broadcasted_iota(jnp.int32, shape, k).astype(jnp.float32)
        grid_ref[k, :, :, 0:wide, :] = (ext_ref[k] + shift) * UNIT

    def one_row(row, carry):
        z, y = row // side, lax.rem(row, side)
        tile = jnp.concatenate(
            [grid_ref[k, z + 1, y + 1] for k in range(3)], axis=0
        )
        columns = tile.T
        for k in range(3):
            for x in range(side):
                place = k * padded + x + 1
                own_ref[k * side + x] = jnp.broadcast_to(
                    columns[:, place : place + 1], (beads, beads)
                )
        for x in range(side):
            count = counts_ref[z, y, x]

            def one_block(i, inner):
                rows = pl.ds(pl.multiple_of(i * ROWS, ROWS), ROWS)
                own = [own_ref[k * side + x, rows, :] for k in range(3)]
                total = [jnp.zeros((ROWS, beads), jnp.float32) for _ in range(3)]
                for dz in range(3):
                    for dy in range(3):
                        for dx in range(3):
                            apart = [
                                own[k]
                                - grid_ref[k, z + dz, y + dy, x + dx : x + dx + 1, :]
                                for k in range(3)
                            ]
                            distance = (
                                apart[0] * apart[0] + apart[1] * apart[1] + apart[2] * apart[2]
                            )
                            weight = jnp.exp(-distance)
                            total = [total[k] + weight * apart[k] for k in range(3)]
                for k in range(3):
                    sum_ref[k * side + x, rows, :] = total[k]
                return inner

            lax.fori_loop(0, (count + (ROWS - 1)) // ROWS, one_block, 0)
        lane = lax.broadcasted_iota(jnp.int32, (1, beads), 1)
        for x in range(side):
            count = counts_ref[z, y, x]
            parts = split_three(
                jnp.concatenate(
                    [grid_ref[k, z + 1, y + 1, x + 1 : x + 2, :] for k in range(3)]
                    + [jnp.zeros((5, beads), jnp.float32)],
                    axis=0,
                )
            )
            stacked = jnp.concatenate(parts + [jnp.zeros((8, beads), jnp.float32)], axis=0)
            product = jnp.dot(
                stacked.astype(jnp.bfloat16), lap_ref[row, x], preferred_element_type=jnp.float32
            )
            bond = product[16:24] + product[8:16] + product[0:8]
            for k in range(3):
                pair = jnp.sum(sum_ref[k * side + x].T, axis=0, keepdims=True)
                force = (STRENGTH / UNIT) * pair - (BOND_STIFF / UNIT) * bond[k : k + 1]
                out_ref[k, z, y, x : x + 1, :] = jnp.where(lane < count, force, 0.0)
        return carry

    lax.fori_loop(0, side * side, one_row, 0)


def bond_matrices(counts, bonds, beads):
    side = counts.shape[0]
    return pl.pallas_call(
        functools.partial(bond_kernel, side),
        out_shape=jax.ShapeDtypeStruct((side * side, side, beads, beads), jnp.bfloat16),
        in_specs=[
            pl.BlockSpec(memory_space=pltpu.SMEM),
            pl.BlockSpec(memory_space=pltpu.VMEM),
        ],
        out_specs=pl.BlockSpec(memory_space=pltpu.VMEM),
        compiler_params=pltpu.CompilerParams(vmem_limit_bytes=40 * 1024 * 1024),
        cost_estimate=pl.CostEstimate(
            flops=2 * side**3 * beads**3, bytes_accessed=2 * side**3 * beads**2, transcendentals=0
        ),
        name="bond_matrices",
    )(counts, bonds)


def local_forces(extended, counts, laps):
    side = counts.shape[0]
    beads = extended.shape[-1]
    wide = side + 2
    padded = -(-wide // 8) * 8
    return pl.pallas_call(
        functools.partial(force_kernel, side),
        out_shape=jax.ShapeDtypeStruct((3, side, side, side, beads), jnp.float32),
        in_specs=[
            pl.BlockSpec(memory_space=pltpu.SMEM),
            pl.BlockSpec(memory_space=pltpu.VMEM),
            pl.BlockSpec(memory_space=pltpu.VMEM),
        ],
        out_specs=pl.BlockSpec(memory_space=pltpu.VMEM),
        scratch_shapes=[
            pltpu.VMEM((3, wide, wide, padded, beads), jnp.float32),
            pltpu.VMEM((3 * side, beads, beads), jnp.float32),
            pltpu.VMEM((3 * side, beads, beads), jnp.float32),
        ],
        compiler_params=pltpu.CompilerParams(vmem_limit_bytes=40 * 1024 * 1024),
        name="cell_forces",
    )(counts, extended, laps)


def halo_extend(parked):
    grown = parked
    for dim, axis in ((1, "gz"), (2, "gy"), (3, "gx")):
        size = grown.shape[dim]
        below = from_behind(lax.slice_in_dim(grown, size - 1, size, axis=dim), axis, 1)
        above = from_behind(lax.slice_in_dim(grown, 0, 1, axis=dim), axis, -1)
        grown = jnp.concatenate([below, grown, above], axis=dim)
    return grown


def pick_entry(plan_table, position):
    matched = jnp.arange(plan_table.shape[0], dtype=jnp.int32) == position
    return jnp.sum(
        jnp.where(matched.reshape((-1,) + (1,) * (plan_table.ndim - 1)), plan_table, 0), axis=0
    )


def hand_over(blocks, arrival, which_axis, lowered, raised, side_cells):
    joined = jnp.concatenate([blocks, arrival, jnp.zeros_like(arrival)], axis=which_axis)
    kept_part = lax.dynamic_slice_in_dim(joined, lowered, side_cells + 2, axis=which_axis)
    filled = side_cells + raised - lowered
    usable = (jnp.arange(side_cells + 2, dtype=jnp.int32) < filled).astype(jnp.float32)
    shape_list = [1] * blocks.ndim
    shape_list[which_axis] = side_cells + 2
    return kept_part * usable.reshape(shape_list)


def on_device(positions, velocities, counts, bonds, plan_z, plan_y, plan_x):
    side_cells = positions.shape[1]
    bead_count = positions.shape[-1]
    living = (jnp.arange(bead_count, dtype=jnp.int32) < counts[..., None]).astype(jnp.float32)
    laps = bond_matrices(counts, bonds, bead_count)
    parked = jnp.where(living[None] > 0, positions, FAR_AWAY)
    forces_first = local_forces(halo_extend(parked), counts, laps)
    stepped = positions + STEP_DT * velocities + 0.5 * STEP_DT * STEP_DT * forces_first
    parked = jnp.where(living[None] > 0, stepped, FAR_AWAY)
    forces_next = local_forces(halo_extend(parked), counts, laps)
    carried = jnp.concatenate([stepped * living[None], forces_next], axis=0)
    plane_index = lax.axis_index("gz")
    column_index = lax.axis_index("gy")
    brick_index = lax.axis_index("gx")
    plane_total = lax.axis_size("gz")
    column_total = lax.axis_size("gy")
    brick_total = lax.axis_size("gx")
    lowered_z = pick_entry(plan_z, (plane_index + plane_total - 1) % plane_total)
    raised_z = pick_entry(plan_z, plane_index)
    plane_row = pick_entry(plan_y, plane_index)
    lowered_y = pick_entry(plane_row, (column_index + column_total - 1) % column_total)
    raised_y = pick_entry(plane_row, column_index)
    column_row = pick_entry(pick_entry(plan_x, plane_index), column_index)
    lowered_x = pick_entry(column_row, (brick_index + brick_total - 1) % brick_total)
    raised_x = pick_entry(column_row, brick_index)
    arrival = from_behind(lax.slice_in_dim(carried, 0, 2, axis=1), "gz", -1)
    carried = hand_over(carried, arrival, 1, lowered_z, raised_z, side_cells)
    arrival = from_behind(lax.slice_in_dim(carried, 0, 2, axis=2), "gy", -1)
    carried = hand_over(carried, arrival, 2, lowered_y, raised_y, side_cells)
    arrival = from_behind(lax.slice_in_dim(carried, 0, 2, axis=3), "gx", -1)
    carried = hand_over(carried, arrival, 3, lowered_x, raised_x, side_cells)
    return (forces_first, carried[:3], carried[3:])


def solution(mesh):
    return jax.shard_map(
        on_device,
        mesh=mesh,
        in_specs=(
            P(None, "gz", "gy", "gx", None),
            P(None, "gz", "gy", "gx", None),
            P("gz", "gy", "gx"),
            P(None, "gz", "gy", "gx", None),
            P(),
            P(),
            P(),
        ),
        out_specs=(
            P(None, "gz", "gy", "gx", None),
            P(None, "gz", "gy", "gx", None),
            P(None, "gz", "gy", "gx", None),
        ),
        check_vma=False,
    )
```
